32 devices in a mesh: groups: 2 (over x), feat: 8 (over z, y), tok: 2 (over core).
Axes of the slice: x: 2, y: 2, z: 4, core: 2. Of those that a mesh axis runs over, the one named last changes fastest.
Arguments:
- activations: bfloat16 [16384, 2048], P(('groups', 'feat'), 'tok'), parts along dimension 0, may hold values from -6 to 6
Outputs:
- hessian: float32 [16384, 8192], P(('groups', 'feat'), 'tok'), parts along dimension 0
The draws below stay inside these ranges and needn't reach their ends.
There are 2 independent parts, one for each index of `groups`. The reference program is written for one: setup_inputs(seed, part) draws one part's arguments, and reference() takes and returns one part's arrays. A program takes and returns all parts, laid end to end along the dimension named above; each array names one. Nothing has to cross between parts.
All inputs are finite; a program needn't handle non-finite values.
Results may differ from the reference program's by a relative error of at most 0.0003.
Values may be sent and summed in bfloat16 or wider, within the bound.
A program may use at most 192 MiB of HBM per device.

```python
import jax
import jax.numpy as jnp

D = 8192
TOKENS = 2048


def block_levels(key, dims, split, smallest, top_value):
    def one(axis_at, parts):
        draws = jax.random.uniform(jax.random.fold_in(jax.random.fold_in(key, 6), axis_at), (parts,), jnp.float32, smallest / len(split), top_value / len(split))
        return jnp.repeat(jnp.exp(draws), dims[axis_at] // parts).reshape((-1,) + (1,) * (len(dims) - axis_at - 1))

    loudness = one(*split[0])
    for cut in split[1:]:
        loudness = loudness * one(*cut)
    return loudness


def scatter_about(rng, shape, deviation, limit, cuts=(), held_as=jnp.bfloat16):
    loudness = block_levels(rng, shape, cuts, -0.22, 0.18) if cuts else 1.0
    result = jax.random.normal(rng, shape, jnp.float32) * deviation * loudness
    return jnp.minimum(jnp.maximum(result, -limit), limit).astype(held_as)


def setup_inputs(seed: int = 0, part: int = 0) -> dict:
    arg_keys = jax.random.split(jax.random.key(seed), 2)
    part_splits = jax.random.split(jax.random.fold_in(arg_keys[1], part), 2)
    return {
        "activations": scatter_about(part_splits[0], (D, TOKENS), 1.0, 6.0, ((0, 8), (1, 2))),
    }


def reference(activations):
    gram = jnp.dot(activations, activations.T, preferred_element_type=jnp.float32)
    return (2.0 / TOKENS) * gram
```

```python
import functools

import jax
import jax.numpy as jnp
from jax import lax
from jax.experimental import pallas as pl
from jax.experimental.pallas import tpu as pltpu
from jax.sharding import PartitionSpec as P

MESH = pl.DeviceIdType.MESH
CHUNK = 64
TILE = 256
SHIFTED = 3
WINDOW = 3
LAG = 4


def kernel(planes, ys, cores, x_ref, o_ref, panels, sib, mate, stage,
           in_sem, out_sem, recv, sib_recv, mate_send, mate_recv, link_send, sib_send):
    n, rows, _ = panels.shape
    per = n // cores
    chunks = rows // CHUNK
    group = TILE // CHUNK
    shifted = SHIFTED if ys > 1 else 0
    ring = ys == 1
    factor = 2.0 / (panels.shape[2] * cores)

    me = lax.axis_index("feat")
    core = lax.axis_index("tok")
    z, y = me // ys, me % ys

    def at(plane, col):
        return lax.rem(plane + planes, planes) * ys + col

    def select(flag, a, b):
        return tuple(jnp.where(flag, i, j) for i, j in zip(a, b))

    if ring:
        counts = {1: (planes // 2,) * 2, -1: (planes - 1 - planes // 2,) * 2}
        most = planes // 2
    else:
        counts = {
            1: (planes - 1 - z, jnp.where(z > 0, planes - z, 0)),
            -1: (z, jnp.where(z < planes - 1, z + 1, 0)),
        }
        most = planes - 1

    def z_item(sign, first, count, t):
        t1 = jnp.maximum(t, 0)
        a = (at(z + sign * (first + t1 // chunks), y), t1 % chunks)
        if shifted:
            t2 = jnp.maximum(t - count * chunks, 0)
            b = (at(z + sign * (first + t2 // shifted), 1 - y), t2 % shifted)
            a = select(t < count * chunks, a, b)
        return (t >= 0) & (t < count * (chunks + shifted)), a[0], a[1]

    def y_item(col, t):
        rest = chunks - shifted
        v = jnp.maximum(t - chunks, 0)
        turn = jnp.where(z < planes // 2, 1, -1)
        far = (at(z + turn * (1 + v // rest), col), shifted + v % rest)
        i, c = select(t < chunks, (at(z, col), jnp.maximum(t, 0)), far)
        return (t >= 0) & (t < chunks + (planes - 1) * rest), i, c

    def sends(link, t):
        return y_item(y, t) if link == 2 else z_item((1, -1)[link], 0, counts[(1, -1)[link]][1], t)

    def arrivals(link, t):
        return y_item(1 - y, t) if link == 2 else z_item((1, -1)[link], 1, counts[(1, -1)[link]][0], t)

    links = (0, 1, 2) if ys > 1 else (0, 1)
    target = (at(z - 1, y), at(z + 1, y), at(z, 1 - y))

    def piece(i, c):
        return panels.at[i, pl.ds(pl.multiple_of(c * CHUNK, CHUNK), CHUNK)]

    def link_copy(link, t, i, c):
        return pltpu.make_async_remote_copy(
            piece(i, c), piece(i, c), link_send.at[link, t % WINDOW], recv.at[i, c],
            device_id={"feat": target[link]}, device_id_type=MESH)

    def sib_copy(link, t, i, c):
        there = sib.at[i % per, pl.ds(pl.multiple_of(c * CHUNK, CHUNK), CHUNK)]
        return pltpu.make_async_remote_copy(
            piece(i, c), there, sib_send.at[link, t % WINDOW], sib_recv.at[i % per, c],
            device_id={"tok": 1 - core}, device_id_type=MESH)

    def mate_copy():
        return pltpu.make_async_remote_copy(
            panels.at[me], mate, mate_send, mate_recv,
            device_id={"tok": 1 - core}, device_id_type=MESH)

    def mine(i):
        return i // per == core

    def tile(i, g, own):
        cols = pl.ds(pl.multiple_of(g * TILE, TILE), TILE)
        if not own:
            for q in range(group):
                sib_copy(0, 0, i, g * group + q).wait_recv()
        other = mate.at[cols] if own else sib.at[i % per, cols]
        a, b = panels[i, cols], other[...]

        @pl.loop(0, rows // TILE)
        def _(r):
            block = pl.ds(pl.multiple_of(r * TILE, TILE), TILE)
            nt = (((1,), (1,)), ((), ()))
            total = lax.dot_general(panels[me, block], a, nt, preferred_element_type=jnp.float32)
            total += lax.dot_general(mate[block], b, nt, preferred_element_type=jnp.float32)
            stage[block] = total * factor

        out = pl.ds(pl.multiple_of((i % per) * rows + g * TILE, TILE), TILE)
        copy = pltpu.make_async_copy(stage, o_ref.at[:, out], out_sem)
        copy.start()
        copy.wait()

    load = pltpu.make_async_copy(x_ref, panels.at[me], in_sem)
    load.start()
    barrier = pltpu.get_barrier_semaphore()
    pl.semaphore_signal(barrier, inc=1, device_id={"tok": 1 - core}, device_id_type=MESH)
    greeted = 1
    for link in links:
        if ring or link == 2:
            pl.semaphore_signal(barrier, inc=1, device_id={"feat": target[link]}, device_id_type=MESH)
            greeted = greeted + 1
        else:
            there = (z > 0, z < planes - 1)[link]

            @pl.when(there)
            def _():
                pl.semaphore_signal(barrier, inc=1, device_id={"feat": target[link]}, device_id_type=MESH)

            greeted = greeted + there.astype(jnp.int32)
    load.wait()
    pl.semaphore_wait(barrier, greeted)

    steps = most * (chunks + shifted)
    if ys > 1:
        steps = max(steps, chunks + (planes - 1) * (chunks - shifted))

    @pl.loop(0, steps + LAG + WINDOW)
    def _(s):
        for link in links:
            past, i, c = sends(link, s - WINDOW)

            @pl.when(past)
            def _():
                link_copy(link, s, i, c).wait_send()

            now, i, c = sends(link, s)

            @pl.when(now)
            def _():
                link_copy(link, s, i, c).start()

        @pl.when(s == 0)
        def _():
            mate_copy().start()

        @pl.when(s == LAG)
        def _():
            mate_copy().wait()

        for link in links:
            past, i, c = arrivals(link, s - LAG - WINDOW)

            @pl.when(past & ~mine(i))
            def _():
                sib_copy(link, s, i, c).wait_send()

            now, i, c = arrivals(link, s - LAG)

            @pl.when(now)
            def _():
                link_copy(link, 0, i, c).wait_recv()

            @pl.when(now & ~mine(i))
            def _():
                sib_copy(link, s, i, c).start()

        own_group = s - 2 * LAG

        @pl.when((own_group >= 0) & (own_group < rows // TILE) & mine(me))
        def _():
            tile(me, own_group, True)

        for link in links:
            now, i, c = arrivals(link, s - LAG)
            ready = now & mine(i) & (c % group == group - 1)
            if shifted:
                whole = (i % ys == y) | (i // ys == z) | (c // group * group >= shifted)
                ready = ready & whole

            @pl.when(ready)
            def _():
                tile(i, c // group, False)

    if shifted:
        @pl.loop(0, planes)
        def _(k):
            i = k * ys + 1 - y

            @pl.when(mine(i) & (k != z))
            def _():
                for g in range(pl.cdiv(shifted, group)):
                    tile(i, g, False)


def shards(planes, ys, cores, activations):
    rows, depth = activations.shape
    n = planes * ys
    per = n // cores
    chunks = rows // CHUNK
    dma = pltpu.SemaphoreType.DMA
    return pl.pallas_call(
        functools.partial(kernel, planes, ys, cores),
        out_shape=jax.ShapeDtypeStruct((rows, per * rows), jnp.float32),
        in_specs=[pl.BlockSpec(memory_space=pl.ANY)],
        out_specs=pl.BlockSpec(memory_space=pl.ANY),
        scratch_shapes=[
            pltpu.VMEM((n, rows, depth), jnp.bfloat16),
            pltpu.VMEM((per, rows, depth), jnp.bfloat16),
            pltpu.VMEM((rows, depth), jnp.bfloat16),
            pltpu.VMEM((rows, TILE), jnp.float32),
            dma, dma, dma((n, chunks)), dma((per, chunks)), dma, dma,
            dma((3, WINDOW)), dma((3, WINDOW)),
        ],
        compiler_params=pltpu.CompilerParams(
            collective_id=0, has_side_effects=True, vmem_limit_bytes=40 * 2**20),
        cost_estimate=pl.CostEstimate(
            flops=2 * rows * per * rows * depth * cores,
            bytes_accessed=4 * rows * per * rows, transcendentals=0),
    )(activations)


def solution(mesh):
    n, cores = mesh.shape["feat"], mesh.shape["tok"]
    ys = 2 if n == 8 else 1
    spec = P(("groups", "feat"), "tok")
    return jax.shard_map(
        functools.partial(shards, n // ys, ys, cores),
        mesh=mesh, in_specs=(spec,), out_specs=spec, check_vma=False)
```

```python
import functools

import jax
import jax.numpy as jnp
from jax import lax
from jax.experimental import pallas as pl
from jax.experimental.pallas import tpu as pltpu
from jax.sharding import PartitionSpec as P

MESH = pl.DeviceIdType.MESH
CHUNK = 64
TILE = 256
SHIFTED = 3
WINDOW = 3
LAG = 4


def kernel(planes, ys, cores, x_ref, o_ref, panels, sib, mate,
           in_sem, recv, sib_recv, mate_send, mate_recv, link_send, sib_send):
    n, rows, _ = panels.shape
    per = n // cores
    chunks = rows // CHUNK
    group = TILE // CHUNK
    shifted = SHIFTED if ys > 1 else 0
    ring = ys == 1
    factor = 2.0 / (panels.shape[2] * cores)

    me = lax.axis_index("feat")
    core = lax.axis_index("tok")
    z, y = me // ys, me % ys

    def at(plane, col):
        return lax.rem(plane + planes, planes) * ys + col

    def select(flag, a, b):
        return tuple(jnp.where(flag, i, j) for i, j in zip(a, b))

    if ring:
        counts = {1: (planes // 2,) * 2, -1: (planes - 1 - planes // 2,) * 2}
        most = planes // 2
    else:
        counts = {
            1: (planes - 1 - z, jnp.where(z > 0, planes - z, 0)),
            -1: (z, jnp.where(z < planes - 1, z + 1, 0)),
        }
        most = planes - 1

    def z_length(count):
        short = jnp.where(count == planes - 1, 1, 0) if shifted else 0
        return count * (chunks + shifted) - short

    rest = chunks - shifted
    y_regular = chunks + (planes - 1) * rest
    turn = jnp.where(z < planes // 2, 1, -1)
    at_end = (z == 0) | (z == planes - 1)
    y_length = y_regular + at_end.astype(jnp.int32)

    def z_item(sign, first, count, t):
        t1 = jnp.maximum(t, 0)
        a = (at(z + sign * (first + t1 // chunks), y), t1 % chunks)
        if shifted:
            t2 = jnp.maximum(t - count * chunks, 0)
            b = (at(z + sign * (first + t2 // shifted), 1 - y), t2 % shifted)
            a = select(t < count * chunks, a, b)
        return (t >= 0) & (t < z_length(count)), a[0], a[1]

    def y_item(col, t):
        v = jnp.maximum(t - chunks, 0)
        far = (at(z + turn * (1 + v // rest), col), shifted + v % rest)
        far = select(t < y_regular, far, (at(z - turn, col), shifted - 1))
        i, c = select(t < chunks, (at(z, col), jnp.maximum(t, 0)), far)
        return (t >= 0) & (t < y_length), i, c

    def sends(link, t):
        return y_item(y, t) if link == 2 else z_item((1, -1)[link], 0, counts[(1, -1)[link]][1], t)

    def arrivals(link, t):
        return y_item(1 - y, t) if link == 2 else z_item((1, -1)[link], 1, counts[(1, -1)[link]][0], t)

    links = (0, 1, 2) if ys > 1 else (0, 1)
    target = (at(z - 1, y), at(z + 1, y), at(z, 1 - y))

    def piece(i, c):
        return panels.at[i, pl.ds(pl.multiple_of(c * CHUNK, CHUNK), CHUNK)]

    def link_copy(link, t, i, c):
        return pltpu.make_async_remote_copy(
            piece(i, c), piece(i, c), link_send.at[link, t % WINDOW], recv.at[i, c],
            device_id={"feat": target[link]}, device_id_type=MESH)

    def sib_copy(link, t, i, c):
        there = sib.at[i % per, pl.ds(pl.multiple_of(c * CHUNK, CHUNK), CHUNK)]
        return pltpu.make_async_remote_copy(
            piece(i, c), there, sib_send.at[link, t % WINDOW], sib_recv.at[i % per, c],
            device_id={"tok": 1 - core}, device_id_type=MESH)

    def mate_copy():
        return pltpu.make_async_remote_copy(
            panels.at[me], mate, mate_send, mate_recv,
            device_id={"tok": 1 - core}, device_id_type=MESH)

    def mine(i):
        return i // per == core

    def tile(i, g, own):
        cols = pl.ds(pl.multiple_of(g * TILE, TILE), TILE)
        if not own:
            for q in range(group):
                sib_copy(0, 0, i, g * group + q).wait_recv()
        other = mate.at[cols] if own else sib.at[i % per, cols]
        a, b = panels[i, cols], other[...]
        out = pl.ds(pl.multiple_of((i % per) * rows + g * TILE, TILE), TILE)

        @pl.loop(0, rows // TILE)
        def _(r):
            block = pl.ds(pl.multiple_of(r * TILE, TILE), TILE)
            nt = (((1,), (1,)), ((), ()))
            total = lax.dot_general(panels[me, block], a, nt, preferred_element_type=jnp.float32)
            total += lax.dot_general(mate[block], b, nt, preferred_element_type=jnp.float32)
            o_ref[block, out] = total * factor

    load = pltpu.make_async_copy(x_ref, panels.at[me], in_sem)
    load.start()
    barrier = pltpu.get_barrier_semaphore()
    pl.semaphore_signal(barrier, inc=1, device_id={"tok": 1 - core}, device_id_type=MESH)
    greeted = 1
    for link in links:
        if ring or link == 2:
            pl.semaphore_signal(barrier, inc=1, device_id={"feat": target[link]}, device_id_type=MESH)
            greeted = greeted + 1
        else:
            there = (z > 0, z < planes - 1)[link]

            @pl.when(there)
            def _():
                pl.semaphore_signal(barrier, inc=1, device_id={"feat": target[link]}, device_id_type=MESH)

            greeted = greeted + there.astype(jnp.int32)
    load.wait()
    pl.semaphore_wait(barrier, greeted)

    steps = most * (chunks + shifted)
    if ys > 1:
        steps = max(steps - 1, y_regular + 1)

    @pl.loop(0, steps + LAG + WINDOW)
    def _(s):
        for link in links:
            past, i, c = sends(link, s - WINDOW)

            @pl.when(past)
            def _():
                link_copy(link, s, i, c).wait_send()

            now, i, c = sends(link, s)

            @pl.when(now)
            def _():
                link_copy(link, s, i, c).start()

        @pl.when(s == 0)
        def _():
            mate_copy().start()

        @pl.when(s == LAG)
        def _():
            mate_copy().wait()

        for link in links:
            past, i, c = arrivals(link, s - LAG - WINDOW)

            @pl.when(past & ~mine(i))
            def _():
                sib_copy(link, s, i, c).wait_send()

            now, i, c = arrivals(link, s - LAG)

            @pl.when(now)
            def _():
                link_copy(link, 0, i, c).wait_recv()

            @pl.when(now & ~mine(i))
            def _():
                sib_copy(link, s, i, c).start()

        own_group = s - 2 * LAG

        @pl.when((own_group >= 0) & (own_group < rows // TILE) & mine(me))
        def _():
            tile(me, own_group, True)

        for link in links:
            now, i, c = arrivals(link, s - LAG)
            ready = now & mine(i) & (c % group == group - 1)
            if shifted:
                whole = (i % ys == y) | (i // ys == z) | (c // group * group >= shifted)
                ready = ready & whole

            @pl.when(ready)
            def _():
                tile(i, c // group, False)

        for p in range(planes // cores if shifted else 0):
            k = core * (planes // cores) + p
            away = jnp.abs(k - z)
            count = jnp.where(k > z, counts[1][0], counts[-1][0])
            by_z = jnp.minimum(count * chunks + away * shifted, z_length(count)) - 1
            turns = lax.rem((k - z) * turn + planes, planes) - 1
            by_y = chunks + turns * rest + group - 1 - shifted
            by_y = jnp.where(away == planes - 1, y_length - 1, by_y)

            @pl.when((k != z) & (s - LAG == jnp.maximum(by_z, by_y)))
            def _():
                tile(k * ys + 1 - y, 0, False)


def shards(planes, ys, cores, activations):
    rows, depth = activations.shape
    n = planes * ys
    per = n // cores
    chunks = rows // CHUNK
    dma = pltpu.SemaphoreType.DMA
    return pl.pallas_call(
        functools.partial(kernel, planes, ys, cores),
        out_shape=pltpu.VMEM((rows, per * rows), jnp.float32),
        in_specs=[pl.BlockSpec(memory_space=pltpu.HBM)],
        out_specs=pl.BlockSpec(memory_space=pltpu.VMEM),
        scratch_shapes=[
            pltpu.VMEM((n, rows, depth), jnp.bfloat16),
            pltpu.VMEM((per, rows, depth), jnp.bfloat16),
            pltpu.VMEM((rows, depth), jnp.bfloat16),
            dma, dma((n, chunks)), dma((per, chunks)), dma, dma,
            dma((3, WINDOW)), dma((3, WINDOW)),
        ],
        compiler_params=pltpu.CompilerParams(
            collective_id=0, has_side_effects=True, vmem_limit_bytes=32 * 2**20),
        cost_estimate=pl.CostEstimate(
            flops=2 * rows * per * rows * depth * cores,
            bytes_accessed=4 * rows * per * rows, transcendentals=0),
    )(pltpu.with_memory_space_constraint(activations, pltpu.HBM))


def solution(mesh):
    n, cores = mesh.shape["feat"], mesh.shape["tok"]
    ys = 2 if n == 8 else 1
    spec = P(("groups", "feat"), "tok")
    return jax.shard_map(
        functools.partial(shards, n // ys, ys, cores),
        mesh=mesh, in_specs=(spec,), out_specs=spec, check_vma=False)
```

```python
import functools

import jax
import jax.numpy as jnp
from jax import lax
from jax.experimental import pallas as pl
from jax.experimental.pallas import tpu as pltpu
from jax.sharding import PartitionSpec as P

MESH = pl.DeviceIdType.MESH
CHUNK = 64
TILE = 256
SHIFTED = 3
WINDOW = 3
LAG = 3


def kernel(planes, ys, cores, x_ref, o_ref, panels, sib, mate,
           in_sem, recv, sib_recv, mate_send, mate_recv, link_send, sib_send):
    n, rows, _ = panels.shape
    per = n // cores
    chunks = rows // CHUNK
    group = TILE // CHUNK
    shifted = SHIFTED if ys > 1 else 0
    ring = ys == 1
    factor = 2.0 / (panels.shape[2] * cores)

    me = lax.axis_index("feat")
    core = lax.axis_index("tok")
    z, y = me // ys, me % ys

    def at(plane, col):
        return lax.rem(plane + planes, planes) * ys + col

    def select(flag, a, b):
        return tuple(jnp.where(flag, i, j) for i, j in zip(a, b))

    if ring:
        counts = {1: (planes // 2,) * 2, -1: (planes - 1 - planes // 2,) * 2}
        most = planes // 2
    else:
        counts = {
            1: (planes - 1 - z, jnp.where(z > 0, planes - z, 0)),
            -1: (z, jnp.where(z < planes - 1, z + 1, 0)),
        }
        most = planes - 1

    def z_length(count):
        short = jnp.where(count == planes - 1, 1, 0) if shifted else 0
        return count * (chunks + shifted) - short

    rest = chunks - shifted
    y_regular = chunks + (planes - 1) * rest
    turn = jnp.where(z < planes // 2, 1, -1)
    at_end = (z == 0) | (z == planes - 1)
    y_length = y_regular + at_end.astype(jnp.int32)

    def z_item(sign, first, count, t):
        t1 = jnp.maximum(t, 0)
        a = (at(z + sign * (first + t1 // chunks), y), t1 % chunks)
        if shifted:
            t2 = jnp.maximum(t - count * chunks, 0)
            b = (at(z + sign * (first + t2 // shifted), 1 - y), t2 % shifted)
            a = select(t < count * chunks, a, b)
        return (t >= 0) & (t < z_length(count)), a[0], a[1]

    def y_item(col, t):
        v = jnp.maximum(t - chunks, 0)
        far = (at(z + turn * (1 + v // rest), col), shifted + v % rest)
        far = select(t < y_regular, far, (at(z - turn, col), shifted - 1))
        i, c = select(t < chunks, (at(z, col), jnp.maximum(t, 0)), far)
        return (t >= 0) & (t < y_length), i, c

    def sends(link, t):
        return y_item(y, t) if link == 2 else z_item((1, -1)[link], 0, counts[(1, -1)[link]][1], t)

    def arrivals(link, t):
        return y_item(1 - y, t) if link == 2 else z_item((1, -1)[link], 1, counts[(1, -1)[link]][0], t)

    links = (0, 1, 2) if ys > 1 else (0, 1)
    target = (at(z - 1, y), at(z + 1, y), at(z, 1 - y))

    def piece(i, c):
        return panels.at[i, pl.ds(pl.multiple_of(c * CHUNK, CHUNK), CHUNK)]

    def link_copy(link, t, i, c):
        return pltpu.make_async_remote_copy(
            piece(i, c), piece(i, c), link_send.at[link, t % WINDOW], recv.at[i, c],
            device_id={"feat": target[link]}, device_id_type=MESH)

    def sib_copy(link, t, i, c):
        there = sib.at[i % per, pl.ds(pl.multiple_of(c * CHUNK, CHUNK), CHUNK)]
        return pltpu.make_async_remote_copy(
            piece(i, c), there, sib_send.at[link, t % WINDOW], sib_recv.at[i % per, c],
            device_id={"tok": 1 - core}, device_id_type=MESH)

    def mate_copy():
        return pltpu.make_async_remote_copy(
            panels.at[me], mate, mate_send, mate_recv,
            device_id={"tok": 1 - core}, device_id_type=MESH)

    def mine(i):
        return i // per == core

    def tile(i, g, own):
        cols = pl.ds(pl.multiple_of(g * TILE, TILE), TILE)
        if not own:
            for q in range(group):
                sib_copy(0, 0, i, g * group + q).wait_recv()
        other = mate.at[cols] if own else sib.at[i % per, cols]
        a, b = panels[i, cols], other[...]
        out = pl.ds(pl.multiple_of((i % per) * rows + g * TILE, TILE), TILE)

        @pl.loop(0, rows // TILE)
        def _(r):
            block = pl.ds(pl.multiple_of(r * TILE, TILE), TILE)
            nt = (((1,), (1,)), ((), ()))
            total = lax.dot_general(panels[me, block], a, nt, preferred_element_type=jnp.float32)
            total += lax.dot_general(mate[block], b, nt, preferred_element_type=jnp.float32)
            o_ref[block, out] = total * factor

    load = pltpu.make_async_copy(x_ref, panels.at[me], in_sem)
    load.start()
    barrier = pltpu.get_barrier_semaphore()
    pl.semaphore_signal(barrier, inc=1, device_id={"tok": 1 - core}, device_id_type=MESH)
    greeted = 1
    for link in links:
        if ring or link == 2:
            pl.semaphore_signal(barrier, inc=1, device_id={"feat": target[link]}, device_id_type=MESH)
            greeted = greeted + 1
        else:
            there = (z > 0, z < planes - 1)[link]

            @pl.when(there)
            def _():
                pl.semaphore_signal(barrier, inc=1, device_id={"feat": target[link]}, device_id_type=MESH)

            greeted = greeted + there.astype(jnp.int32)
    load.wait()
    pl.semaphore_wait(barrier, greeted)

    steps = most * (chunks + shifted)
    if ys > 1:
        steps = max(steps - 1, y_regular + 1)

    @pl.loop(0, steps + max(LAG + 1, WINDOW))
    def _(s):
        for link in links:
            past, i, c = sends(link, s - WINDOW)

            @pl.when(past)
            def _():
                link_copy(link, s, i, c).wait_send()

            now, i, c = sends(link, s)

            @pl.when(now)
            def _():
                link_copy(link, s, i, c).start()

        @pl.when(s == 0)
        def _():
            mate_copy().start()

        @pl.when(s == LAG)
        def _():
            mate_copy().wait()

        for link in links:
            past, i, c = arrivals(link, s - LAG - 1)

            @pl.when(past & ~mine(i))
            def _():
                sib_copy(link, s - 1, i, c).wait_send()

            now, i, c = arrivals(link, s - LAG)

            @pl.when(now)
            def _():
                link_copy(link, 0, i, c).wait_recv()

            @pl.when(now & ~mine(i))
            def _():
                sib_copy(link, s, i, c).start()

        own_group = s - 2 * LAG

        @pl.when((own_group >= 0) & (own_group < rows // TILE) & mine(me))
        def _():
            tile(me, own_group, True)

        for link in links:
            now, i, c = arrivals(link, s - LAG)
            ready = now & mine(i) & (c % group == group - 1)
            if shifted:
                whole = (i % ys == y) | (i // ys == z) | (c // group * group >= shifted)
                ready = ready & whole

            @pl.when(ready)
            def _():
                tile(i, c // group, False)

        for p in range(planes // cores if shifted else 0):
            k = core * (planes // cores) + p
            away = jnp.abs(k - z)
            count = jnp.where(k > z, counts[1][0], counts[-1][0])
            by_z = jnp.minimum(count * chunks + away * shifted, z_length(count)) - 1
            turns = lax.rem((k - z) * turn + planes, planes) - 1
            by_y = chunks + turns * rest + group - 1 - shifted
            by_y = jnp.where(away == planes - 1, y_length - 1, by_y)

            @pl.when((k != z) & (s - LAG == jnp.maximum(by_z, by_y)))
            def _():
                tile(k * ys + 1 - y, 0, False)


def shards(planes, ys, cores, activations):
    rows, depth = activations.shape
    n = planes * ys
    per = n // cores
    chunks = rows // CHUNK
    dma = pltpu.SemaphoreType.DMA
    return pl.pallas_call(
        functools.partial(kernel, planes, ys, cores),
        out_shape=pltpu.VMEM((rows, per * rows), jnp.float32),
        in_specs=[pl.BlockSpec(memory_space=pltpu.HBM)],
        out_specs=pl.BlockSpec(memory_space=pltpu.VMEM),
        scratch_shapes=[
            pltpu.VMEM((n, rows, depth), jnp.bfloat16),
            pltpu.VMEM((per, rows, depth), jnp.bfloat16),
            pltpu.VMEM((rows, depth), jnp.bfloat16),
            dma, dma((n, chunks)), dma((per, chunks)), dma, dma,
            dma((3, WINDOW)), dma((3, WINDOW)),
        ],
        compiler_params=pltpu.CompilerParams(
            collective_id=0, has_side_effects=True, vmem_limit_bytes=32 * 2**20),
        cost_estimate=pl.CostEstimate(
            flops=2 * rows * per * rows * depth * cores,
            bytes_accessed=4 * rows * per * rows, transcendentals=0),
    )(pltpu.with_memory_space_constraint(activations, pltpu.HBM))


def solution(mesh):
    n, cores = mesh.shape["feat"], mesh.shape["tok"]
    ys = 2 if n == 8 else 1
    spec = P(("groups", "feat"), "tok")
    return jax.shard_map(
        functools.partial(shards, n // ys, ys, cores),
        mesh=mesh, in_specs=(spec,), out_specs=spec, check_vma=False)
```

```python
import functools

import jax
import jax.numpy as jnp
from jax import lax
from jax.experimental import pallas as pl
from jax.experimental.pallas import tpu as pltpu
from jax.sharding import PartitionSpec as P

MESH = pl.DeviceIdType.MESH
CHUNK = 64
TILE = 256
BLOCK = 512
SHIFTED = 3
WINDOW = 3
LAG = 3


def kernel(planes, ys, cores, x_ref, o_ref, panels, sib, mate,
           in_sem, recv, sib_recv, mate_send, mate_recv, link_send, sib_send):
    n, rows, _ = panels.shape
    per = n // cores
    chunks = rows // CHUNK
    group = TILE // CHUNK
    shifted = SHIFTED if ys > 1 else 0
    ring = ys == 1
    factor = 2.0 / (panels.shape[2] * cores)

    me = lax.axis_index("feat")
    core = lax.axis_index("tok")
    z, y = me // ys, me % ys

    def at(plane, col):
        return lax.rem(plane + planes, planes) * ys + col

    def select(flag, a, b):
        return tuple(jnp.where(flag, i, j) for i, j in zip(a, b))

    if ring:
        counts = {1: (planes // 2,) * 2, -1: (planes - 1 - planes // 2,) * 2}
        most = planes // 2
    else:
        counts = {
            1: (planes - 1 - z, jnp.where(z > 0, planes - z, 0)),
            -1: (z, jnp.where(z < planes - 1, z + 1, 0)),
        }
        most = planes - 1

    def z_length(count):
        short = jnp.where(count == planes - 1, 1, 0) if shifted else 0
        return count * (chunks + shifted) - short

    rest = chunks - shifted
    y_regular = chunks + (planes - 1) * rest
    turn = jnp.where(z < planes // 2, 1, -1)
    at_end = (z == 0) | (z == planes - 1)
    y_length = y_regular + at_end.astype(jnp.int32)

    def z_item(sign, first, count, t):
        t1 = jnp.maximum(t, 0)
        a = (at(z + sign * (first + t1 // chunks), y), t1 % chunks)
        if shifted:
            t2 = jnp.maximum(t - count * chunks, 0)
            b = (at(z + sign * (first + t2 // shifted), 1 - y), t2 % shifted)
            a = select(t < count * chunks, a, b)
        return (t >= 0) & (t < z_length(count)), a[0], a[1]

    def y_item(col, t):
        v = jnp.maximum(t - chunks, 0)
        far = (at(z + turn * (1 + v // rest), col), shifted + v % rest)
        far = select(t < y_regular, far, (at(z - turn, col), shifted - 1))
        i, c = select(t < chunks, (at(z, col), jnp.maximum(t, 0)), far)
        return (t >= 0) & (t < y_length), i, c

    def sends(link, t):
        return y_item(y, t) if link == 2 else z_item((1, -1)[link], 0, counts[(1, -1)[link]][1], t)

    def arrivals(link, t):
        return y_item(1 - y, t) if link == 2 else z_item((1, -1)[link], 1, counts[(1, -1)[link]][0], t)

    links = (0, 1, 2) if ys > 1 else (0, 1)
    target = (at(z - 1, y), at(z + 1, y), at(z, 1 - y))

    def piece(i, c):
        return panels.at[i, pl.ds(pl.multiple_of(c * CHUNK, CHUNK), CHUNK)]

    def link_copy(link, t, i, c):
        return pltpu.make_async_remote_copy(
            piece(i, c), piece(i, c), link_send.at[link, t % WINDOW], recv.at[i, c],
            device_id={"feat": target[link]}, device_id_type=MESH)

    def sib_copy(link, t, i, c):
        there = sib.at[i % per, pl.ds(pl.multiple_of(c * CHUNK, CHUNK), CHUNK)]
        return pltpu.make_async_remote_copy(
            piece(i, c), there, sib_send.at[link, t % WINDOW], sib_recv.at[i % per, c],
            device_id={"tok": 1 - core}, device_id_type=MESH)

    def mate_copy():
        return pltpu.make_async_remote_copy(
            panels.at[me], mate, mate_send, mate_recv,
            device_id={"tok": 1 - core}, device_id_type=MESH)

    def mine(i):
        return i // per == core

    def tile(i, g, own):
        cols = pl.ds(pl.multiple_of(g * TILE, TILE), TILE)
        if not own:
            for q in range(group):
                sib_copy(0, 0, i, g * group + q).wait_recv()
        other = mate.at[cols] if own else sib.at[i % per, cols]
        a, b = panels[i, cols], other[...]
        out = pl.ds(pl.multiple_of((i % per) * rows + g * TILE, TILE), TILE)

        @pl.loop(0, rows // BLOCK)
        def _(r):
            block = pl.ds(pl.multiple_of(r * BLOCK, BLOCK), BLOCK)
            nt = (((1,), (1,)), ((), ()))
            total = lax.dot_general(panels[me, block], a, nt, preferred_element_type=jnp.float32)
            total += lax.dot_general(mate[block], b, nt, preferred_element_type=jnp.float32)
            o_ref[block, out] = total * factor

    load = pltpu.make_async_copy(x_ref, panels.at[me], in_sem)
    load.start()
    barrier = pltpu.get_barrier_semaphore()
    pl.semaphore_signal(barrier, inc=1, device_id={"tok": 1 - core}, device_id_type=MESH)
    greeted = 1
    for link in links:
        if ring or link == 2:
            pl.semaphore_signal(barrier, inc=1, device_id={"feat": target[link]}, device_id_type=MESH)
            greeted = greeted + 1
        else:
            there = (z > 0, z < planes - 1)[link]

            @pl.when(there)
            def _():
                pl.semaphore_signal(barrier, inc=1, device_id={"feat": target[link]}, device_id_type=MESH)

            greeted = greeted + there.astype(jnp.int32)
    load.wait()
    pl.semaphore_wait(barrier, greeted)

    steps = most * (chunks + shifted)
    if ys > 1:
        steps = max(steps - 1, y_regular + 1)

    @pl.loop(0, steps + max(LAG + 1, WINDOW))
    def _(s):
        for link in links:
            past, i, c = sends(link, s - WINDOW)

            @pl.when(past)
            def _():
                link_copy(link, s, i, c).wait_send()

            now, i, c = sends(link, s)

            @pl.when(now)
            def _():
                link_copy(link, s, i, c).start()

        @pl.when(s == 0)
        def _():
            mate_copy().start()

        @pl.when(s == LAG)
        def _():
            mate_copy().wait()

        for link in links:
            past, i, c = arrivals(link, s - LAG - 1)

            @pl.when(past & ~mine(i))
            def _():
                sib_copy(link, s - 1, i, c).wait_send()

            now, i, c = arrivals(link, s - LAG)

            @pl.when(now)
            def _():
                link_copy(link, 0, i, c).wait_recv()

            @pl.when(now & ~mine(i))
            def _():
                sib_copy(link, s, i, c).start()

        own_group = s - 2 * LAG

        @pl.when((own_group >= 0) & (own_group < rows // TILE) & mine(me))
        def _():
            tile(me, own_group, True)

        for link in links:
            now, i, c = arrivals(link, s - LAG)
            ready = now & mine(i) & (c % group == group - 1)
            if shifted:
                whole = (i % ys == y) | (i // ys == z) | (c // group * group >= shifted)
                ready = ready & whole

            @pl.when(ready)
            def _():
                tile(i, c // group, False)

        for p in range(planes // cores if shifted else 0):
            k = core * (planes // cores) + p
            away = jnp.abs(k - z)
            count = jnp.where(k > z, counts[1][0], counts[-1][0])
            by_z = jnp.minimum(count * chunks + away * shifted, z_length(count)) - 1
            turns = lax.rem((k - z) * turn + planes, planes) - 1
            by_y = chunks + turns * rest + group - 1 - shifted
            by_y = jnp.where(away == planes - 1, y_length - 1, by_y)

            @pl.when((k != z) & (s - LAG == jnp.maximum(by_z, by_y)))
            def _():
                tile(k * ys + 1 - y, 0, False)


def shards(planes, ys, cores, activations):
    rows, depth = activations.shape
    n = planes * ys
    per = n // cores
    chunks = rows // CHUNK
    dma = pltpu.SemaphoreType.DMA
    return pl.pallas_call(
        functools.partial(kernel, planes, ys, cores),
        out_shape=pltpu.VMEM((rows, per * rows), jnp.float32),
        in_specs=[pl.BlockSpec(memory_space=pltpu.HBM)],
        out_specs=pl.BlockSpec(memory_space=pltpu.VMEM),
        scratch_shapes=[
            pltpu.VMEM((n, rows, depth), jnp.bfloat16),
            pltpu.VMEM((per, rows, depth), jnp.bfloat16),
            pltpu.VMEM((rows, depth), jnp.bfloat16),
            dma, dma((n, chunks)), dma((per, chunks)), dma, dma,
            dma((3, WINDOW)), dma((3, WINDOW)),
        ],
        compiler_params=pltpu.CompilerParams(
            collective_id=0, has_side_effects=True, vmem_limit_bytes=32 * 2**20),
        cost_estimate=pl.CostEstimate(
            flops=2 * rows * per * rows * depth * cores,
            bytes_accessed=4 * rows * per * rows, transcendentals=0),
    )(pltpu.with_memory_space_constraint(activations, pltpu.HBM))


def solution(mesh):
    n, cores = mesh.shape["feat"], mesh.shape["tok"]
    ys = 2 if n == 8 else 1
    spec = P(("groups", "feat"), "tok")
    return jax.shard_map(
        functools.partial(shards, n // ys, ys, cores),
        mesh=mesh, in_specs=(spec,), out_specs=spec, check_vma=False)
```
